256 devices in a mesh: file: 2 (over x_hi), seq: 32 (over y, z), tp: 4 (over x_lo, core).
Axes of the slice: x: 4 (x_hi: 2, x_lo: 2; x = x_hi * 2 + x_lo), y: 4, z: 8, core: 2. Of those that a mesh axis runs over, the one named last changes fastest.
Arguments:
- queries: bfloat16 [32768, 4096], P(('file', 'tp', 'seq')), parts along dimension 0
- keys: bfloat16 [32768, 1024], P(('file', 'tp', 'seq')), parts along dimension 0
- values: bfloat16 [32768, 1024], P(('file', 'tp', 'seq')), parts along dimension 0, may hold values from -6 to 6
- mem_pos: int32 [2048], P(('file', 'tp', 'seq')), parts along dimension 0, may hold values from 0 to 16383, as said below
- norm_gain: float32 [4096], replicated, may hold values from 0.1 to 1.9
- summary_weight: bfloat16 [4096, 6144], P('tp', 'seq'), may hold values from -0.09375 to 0.09375
Outputs:
- encoded: bfloat16 [32768, 4096], P(('file', 'tp', 'seq')), parts along dimension 0
- summary: bfloat16 [2048, 6144], P(('file', 'tp'), 'seq'), parts along dimension 0
The draws below stay inside these ranges and needn't reach their ends.
There are 2 independent parts, one for each index of `file`. The reference program is written for one: setup_inputs(seed, part) draws one part's arguments, and reference() takes and returns one part's arrays. A program takes and returns all parts, laid end to end along the dimension named above; an argument that names none is the same for every part. Nothing has to cross between parts.
Inputs may be any that keep to these rules, and one draw needn't show every extreme that they name: `mem_pos`: entry j lies among rows 16 * j to 16 * j + 15.
All inputs are finite; a program needn't handle non-finite values.
Results may differ from the reference program's by a relative error of at most 0.018.
Values may be sent and summed in bfloat16 or wider, within the bound.
No kernel may reach another device: no remote copies, remote signals or barrier semaphores. Data moves between devices by JAX's collectives and lax.ppermute only.
A program may use at most 64 MiB of HBM per device.

```python
import jax
import jax.numpy as jnp
from jax import lax

D = 4096
HEADS = 32
KV_HEADS = 8
HEAD_DIM = 128
GROUP = 16
SEQ_LEN = 16384
WINDOW = 4096
MEM = 1024
QKV_OUT = 6144


def draw_queries(key, part):
    key = jax.random.fold_in(key, 11)
    base = jnp.clip(jax.random.normal(key, (SEQ_LEN, HEADS, HEAD_DIM), jnp.float32), -4.0, 4.0)
    return base.reshape(SEQ_LEN, HEADS * HEAD_DIM).astype(jnp.bfloat16)


def draw_keys(key, part):
    key = jax.random.fold_in(key, 23)
    base = jnp.clip(jax.random.normal(key, (SEQ_LEN, KV_HEADS, HEAD_DIM), jnp.float32), -4.0, 4.0)
    return base.reshape(SEQ_LEN, KV_HEADS * HEAD_DIM).astype(jnp.bfloat16)


def draw_mem_pos(key, part):
    key = jax.random.fold_in(key, 5)
    offsets = jax.random.randint(key, (MEM,), 0, GROUP, dtype=jnp.int32)
    index = jnp.arange(MEM, dtype=jnp.int32)
    offsets = jnp.where(index == 0, 0, offsets)
    offsets = jnp.where(index == MEM - 1, GROUP - 1, offsets)
    return offsets + GROUP * index


def shard_levels(key, extent, cuts, low, top_value):
    level, own = 1.0, jax.random.fold_in(key, 6)
    for position, blocks in cuts:
        steps = jnp.exp(jax.random.uniform(jax.random.fold_in(own, position), (blocks,), jnp.float32, low / len(cuts), top_value / len(cuts)))
        level = level * jnp.repeat(steps, extent[position] // blocks).reshape([-1 if axis == position else 1 for axis in range(len(extent))])
    return level


def scatter_about(key, dims, scale, most, pieces=(), held_as=jnp.bfloat16):
    factor_of = shard_levels(key, dims, pieces, -0.22, 0.18) if pieces else 1.0
    result = jax.random.normal(key, dims, jnp.float32) * scale * factor_of
    return jnp.minimum(jnp.maximum(result, -most), most).astype(held_as)


def setup_inputs(seed: int = 0, part: int = 0) -> dict:
    streams_of = jax.random.split(jax.random.key(seed), 7)
    part_splits = jax.random.split(jax.random.fold_in(streams_of[6], part), 7)
    queries = draw_queries(jax.random.fold_in(jax.random.fold_in(streams_of[6], part), 71), part)
    keys = draw_keys(jax.random.fold_in(jax.random.fold_in(streams_of[6], part), 71), part)
    values = scatter_about(part_splits[2], (SEQ_LEN, KV_HEADS * HEAD_DIM), 1.0, 6.0, ((0, 128),))
    mem_pos = draw_mem_pos(jax.random.fold_in(jax.random.fold_in(streams_of[6], part), 71), part)
    norm_gain = jnp.clip(1.0 + 0.18 * jax.random.normal(streams_of[4], (D,), jnp.float32), 0.1, 1.9)
    summary_weight = scatter_about(streams_of[5], (D, QKV_OUT), D ** -0.5, 0.09375, ((0, 4), (1, 32)))
    return {"queries": queries, "keys": keys, "values": values, "mem_pos": mem_pos, "norm_gain": norm_gain, "summary_weight": summary_weight}


def reference(queries, keys, values, mem_pos, norm_gain, summary_weight):
    group = HEADS // KV_HEADS
    scale = 1.0 / HEAD_DIM ** 0.5
    block = 512 if SEQ_LEN % 512 == 0 else SEQ_LEN
    query_heads = queries.reshape(SEQ_LEN, HEADS, HEAD_DIM)
    key_heads = jnp.pad(keys.reshape(SEQ_LEN, KV_HEADS, HEAD_DIM), ((WINDOW, 0), (0, 0), (0, 0)))
    value_heads = jnp.pad(values.reshape(SEQ_LEN, KV_HEADS, HEAD_DIM), ((WINDOW, 0), (0, 0), (0, 0)))

    def one_head(head):
        kv_index = head // group
        q_head = lax.dynamic_index_in_dim(query_heads, head, 1, keepdims=False)
        k_head = lax.dynamic_index_in_dim(key_heads, kv_index, 1, keepdims=False)
        v_head = lax.dynamic_index_in_dim(value_heads, kv_index, 1, keepdims=False)

        def one_block(index):
            first = (index * block).astype(jnp.int32)
            q_block = lax.dynamic_slice_in_dim(q_head, first, block, 0)
            k_block = lax.dynamic_slice_in_dim(k_head, first, WINDOW + block, 0)
            v_block = lax.dynamic_slice_in_dim(v_head, first, WINDOW + block, 0)
            q_where = first + jnp.arange(block, dtype=jnp.int32)
            k_where = first - WINDOW + jnp.arange(WINDOW + block, dtype=jnp.int32)
            seen = (k_where[None, :] <= q_where[:, None]) & (k_where[None, :] > q_where[:, None] - WINDOW) & (k_where[None, :] >= 0)
            scores = jnp.dot(q_block, k_block.T, preferred_element_type=jnp.float32) * scale
            masked = jnp.where(seen, scores, -jnp.inf)
            peak = lax.optimization_barrier(jnp.max(masked, axis=1, keepdims=True))
            weights = jnp.where(seen, jnp.exp(scores - peak), 0.0)
            total = lax.optimization_barrier(jnp.sum(weights, axis=1, keepdims=True))
            mixed = jnp.dot(weights.astype(jnp.bfloat16), v_block, preferred_element_type=jnp.float32)
            return mixed / total
        parts = lax.map(one_block, jnp.arange(SEQ_LEN // block, dtype=jnp.int32))
        return parts.reshape(SEQ_LEN, HEAD_DIM)
    outputs = lax.map(one_head, jnp.arange(HEADS, dtype=jnp.int32))
    encoded = jnp.transpose(outputs, (1, 0, 2)).reshape(SEQ_LEN, D).astype(jnp.bfloat16)
    picked = jnp.take(encoded, mem_pos.astype(jnp.int32), axis=0).astype(jnp.float32)
    meansq = lax.optimization_barrier(jnp.mean(picked * picked, axis=1, keepdims=True))
    normed = (picked * lax.rsqrt(meansq + 1e-05) * norm_gain[None, :]).astype(jnp.bfloat16)
    summary = jnp.dot(normed, summary_weight, preferred_element_type=jnp.float32).astype(jnp.bfloat16)
    return (encoded, summary)
```

```python
import functools

import jax
import jax.numpy as jnp
from jax import lax
from jax.experimental import pallas as pl
from jax.experimental.pallas import tpu as pltpu
from jax.sharding import Mesh, PartitionSpec as P

D = 4096
HEADS = 32
KV_HEADS = 8
HEAD_DIM = 128
GROUP_HEADS = HEADS // KV_HEADS
ROWS = 128
N_Z = 8
N_Y = 4
SPAN = ROWS * N_Z
WINDOW = 4096
PRIOR = WINDOW // SPAN
TILE = 256
CHUNK = 512
CALLS = 2
COEF = 1.4426950408889634 / HEAD_DIM**0.5
PLACES = ("y", "xl", "core")
GROUPS = 4 * N_Y


def scores_of(q, k):
    return lax.dot_general(q, k, (((1,), (1,)), ((), ())), preferred_element_type=jnp.float32)


def mix(p, v):
    return jnp.dot(p, v, preferred_element_type=jnp.float32)


def attend_kernel(heads, absent_ref, q_ref, *refs):
    pieces, (o_ref, k_all, v_all, q_rows) = refs[: PRIOR + 1], refs[PRIOR + 1 :]
    step = pl.program_id(0)
    blocks = TILE // ROWS
    count = heads * TILE

    @pl.when(step == 0)
    def _():
        for slot, piece in enumerate(pieces):
            for z in range(N_Z):
                at = pl.ds(slot * SPAN + z * ROWS, ROWS)
                k_all[at, :] = piece[z, 0]
                v_all[at, :HEAD_DIM] = piece[z, 1]
                v_all[at, HEAD_DIM:] = jnp.ones((ROWS, HEAD_DIM), jnp.bfloat16)
        absent = absent_ref[0]
        for slot in range(PRIOR):

            @pl.when(slot < absent)
            def _():
                first = k_all[pl.ds(pl.multiple_of(absent * SPAN, SPAN), 16), :][:1, :]
                at = pl.ds(slot * SPAN, SPAN)
                k_all[at, :] = jnp.broadcast_to(first, (SPAN, HEAD_DIM))
                v_all[at, :] = jnp.zeros((SPAN, 2 * HEAD_DIM), jnp.bfloat16)

    for h in range(heads):
        for b in range(blocks):
            q_rows[h * TILE + b * ROWS : h * TILE + (b + 1) * ROWS, :] = q_ref[
                b, :, h * HEAD_DIM : (h + 1) * HEAD_DIM
            ]
    q = q_rows[...]
    start = step * TILE

    def window(ref, offset, size):
        return ref[pl.ds(pl.multiple_of(start + offset, TILE), size), :]

    row = lax.broadcasted_iota(jnp.int32, (1, TILE, TILE), 1)
    col = lax.broadcasted_iota(jnp.int32, (1, TILE, TILE), 2)
    own = col <= row
    oldest = scores_of(q, window(k_all, 0, TILE)).reshape(heads, TILE, TILE)
    newest = scores_of(q, window(k_all, WINDOW, TILE)).reshape(heads, TILE, TILE)
    s = jnp.where(own, newest, oldest).reshape(count, TILE)
    peak = jnp.max(s, axis=1, keepdims=True)
    p = jnp.exp2(s * COEF - peak * COEF).astype(jnp.bfloat16).reshape(heads, TILE, TILE)
    zero = jnp.zeros((), jnp.bfloat16)
    total = mix(jnp.where(own, p, zero).reshape(count, TILE), window(v_all, WINDOW, TILE))
    total += mix(jnp.where(own, zero, p).reshape(count, TILE), window(v_all, 0, TILE))
    offset = TILE
    while offset < WINDOW:
        size = min(CHUNK, WINDOW - offset)
        s = scores_of(q, window(k_all, offset, size))
        higher = jnp.maximum(peak, jnp.max(s, axis=1, keepdims=True))
        fade = jnp.exp2(peak * COEF - higher * COEF)
        p = jnp.exp2(s * COEF - higher * COEF).astype(jnp.bfloat16)
        total = total * fade + mix(p, window(v_all, offset, size))
        peak = higher
        offset += size
    out = (total[:, :HEAD_DIM] / total[:, HEAD_DIM:]).astype(jnp.bfloat16)
    for h in range(heads):
        for b in range(blocks):
            o_ref[b, :, h * HEAD_DIM : (h + 1) * HEAD_DIM] = out[
                h * TILE + b * ROWS : h * TILE + (b + 1) * ROWS, :
            ]


def attend(q, pieces, absent):
    heads = q.shape[2] // HEAD_DIM
    blocks = TILE // ROWS
    rows = pl.BlockSpec((blocks, ROWS, heads * HEAD_DIM), lambda i, a: (i, 0, 0))
    whole = pl.BlockSpec((N_Z, 2, ROWS, HEAD_DIM), lambda i, a: (0, 0, 0, 0))
    return pl.pallas_call(
        functools.partial(attend_kernel, heads),
        grid_spec=pltpu.PrefetchScalarGridSpec(
            num_scalar_prefetch=1,
            grid=(SPAN // TILE,),
            in_specs=[rows] + [whole] * (PRIOR + 1),
            out_specs=rows,
            scratch_shapes=[
                pltpu.VMEM((WINDOW + SPAN, HEAD_DIM), jnp.bfloat16),
                pltpu.VMEM((WINDOW + SPAN, 2 * HEAD_DIM), jnp.bfloat16),
                pltpu.VMEM((heads * TILE, HEAD_DIM), jnp.bfloat16),
            ],
        ),
        out_shape=jax.ShapeDtypeStruct(q.shape, q.dtype),
        compiler_params=pltpu.CompilerParams(vmem_limit_bytes=48 * 2**20),
        cost_estimate=pl.CostEstimate(
            flops=heads * SPAN * WINDOW * HEAD_DIM * 8,
            bytes_accessed=4 * 2**20,
            transcendentals=heads * SPAN * WINDOW,
        ),
    )(absent, q, *pieces)


def to_groups(a, axis="z"):
    return lax.all_to_all(a, axis, split_axis=0, concat_axis=0, tiled=True)


def from_group_behind(a, back):
    def index(group):
        return group % N_Y * (GROUPS // N_Y) + group // N_Y

    return lax.ppermute(a, PLACES, [(index(g - back), index(g)) for g in range(back, GROUPS)])


def on_device(queries, keys, values, mem_pos, norm_gain, summary_weight):
    xl, core, y = lax.axis_index("xl"), lax.axis_index("core"), lax.axis_index("y")
    place = (xl * 2 + core) * N_Y + y

    packed = jnp.stack(
        (keys.reshape(ROWS, KV_HEADS, HEAD_DIM), values.reshape(ROWS, KV_HEADS, HEAD_DIM))
    )
    own = to_groups(jnp.transpose(packed, (2, 0, 1, 3)))
    pieces = [from_group_behind(own, back) for back in range(PRIOR, 0, -1)] + [own]
    absent = jnp.maximum(PRIOR - place, 0).astype(jnp.int32).reshape(1)

    heads = GROUP_HEADS // CALLS
    by_group = jnp.transpose(
        queries.reshape(ROWS, N_Z, CALLS, heads * HEAD_DIM), (2, 1, 0, 3)
    )
    q_parts = [to_groups(by_group[c]) for c in range(CALLS)]

    w_y = [summary_weight] + [
        lax.ppermute(summary_weight, "y", [(i, (i + s) % N_Y) for i in range(N_Y)])
        for s in range(1, N_Y)
    ]
    w_y = jnp.stack(w_y)
    w_x = jnp.stack((w_y, lax.ppermute(w_y, "xl", [(0, 1), (1, 0)])))
    w_all = jnp.stack((w_x, lax.ppermute(w_x, "core", [(0, 1), (1, 0)])))

    sent = [to_groups(attend(q, pieces, absent)) for q in q_parts]
    encoded = jnp.transpose(jnp.stack(sent), (2, 1, 0, 3)).reshape(ROWS, D)

    picked = jnp.take(encoded, mem_pos % ROWS, axis=0).astype(jnp.float32)
    meansq = jnp.mean(picked * picked, axis=1, keepdims=True)
    normed = (picked * lax.rsqrt(meansq + 1e-05) * norm_gain[None, :]).astype(jnp.bfloat16)
    mem_dev = normed.shape[0]
    memory = to_groups(jnp.broadcast_to(normed[None], (N_Z, mem_dev, D)))
    memory = memory.reshape(N_Z * mem_dev, 2, 2, D // 4)
    sums = 0.0
    for c in range(2):
        for x in range(2):
            part = lax.dynamic_slice(
                memory, (0, (xl + x) % 2, (core + c) % 2, 0), (N_Z * mem_dev, 1, 1, D // 4)
            ).reshape(N_Z * mem_dev, D // 4)
            sums += jnp.einsum(
                "rk,ykn->yrn", part, w_all[c, x], preferred_element_type=jnp.float32
            )
    sums = jnp.take(sums.astype(jnp.bfloat16), (y - jnp.arange(N_Y)) % N_Y, axis=0)
    summary = to_groups(sums, "y").reshape(N_Y * N_Z * mem_dev, -1)
    return encoded, summary


def solution(mesh):
    split = Mesh(mesh.devices.reshape(-1, N_Y, N_Z, 2, 2), ("file", "y", "z", "xl", "core"))
    tokens = ("file", "xl", "core", "y", "z")
    return jax.shard_map(
        on_device,
        mesh=split,
        in_specs=(
            P(tokens, None),
            P(tokens, None),
            P(tokens, None),
            P(tokens),
            P(),
            P(("xl", "core"), ("y", "z")),
        ),
        out_specs=(P(tokens, None), P(("file", "xl", "core"), ("y", "z"))),
        check_vma=False,
    )
```

```python
import functools

import jax
import jax.numpy as jnp
from jax import lax
from jax.experimental import pallas as pl
from jax.experimental.pallas import tpu as pltpu
from jax.sharding import Mesh, PartitionSpec as P

D = 4096
HEADS = 32
KV_HEADS = 8
HEAD_DIM = 128
GROUP_HEADS = HEADS // KV_HEADS
GROUP_COLS = GROUP_HEADS * HEAD_DIM
ROWS = 128
MEM_ROWS = 8
STRIDE = ROWS // MEM_ROWS
EXTRA = 16
N_Z = 8
N_Y = 4
SPAN = ROWS * N_Z
SPAN_MEM = MEM_ROWS * N_Z
WINDOW = 4096
REACH = WINDOW + SPAN
PRIOR = WINDOW // SPAN
TILE = 256
CHUNK = 512
CALLS = 2
COEF = 1.4426950408889634 / HEAD_DIM**0.5
VMEM_LIMIT = 20 * 2**20
FIRST_LIMIT = 56 * 2**20
PLACES = ("y", "xl", "core")
GROUPS = 4 * N_Y
SWAP = [(0, 1), (1, 0)]


def scores_of(q, k):
    return lax.dot_general(q, k, (((1,), (1,)), ((), ())), preferred_element_type=jnp.float32)


def mix(p, v):
    return jnp.dot(p, v, preferred_element_type=jnp.float32)


def pack_kv_kernel(k_ref, v_ref, o_ref):
    for g in range(KV_HEADS):
        cols = slice(g * HEAD_DIM, (g + 1) * HEAD_DIM)
        o_ref[g, 0] = k_ref[:, cols]
        o_ref[g, 1] = v_ref[:, cols]


def pack_kv(keys, values):
    return pl.pallas_call(
        pack_kv_kernel,
        out_shape=jax.ShapeDtypeStruct((KV_HEADS, 2, ROWS, HEAD_DIM), keys.dtype),
        compiler_params=pltpu.CompilerParams(vmem_limit_bytes=VMEM_LIMIT),
        cost_estimate=pl.CostEstimate(flops=0, bytes_accessed=2**20, transcendentals=0),
    )(keys, values)


def pack_q_kernel(pos_ref, q_ref, o_ref):
    row = lax.broadcasted_iota(jnp.int32, (EXTRA, ROWS), 0)
    col = lax.broadcasted_iota(jnp.int32, (EXTRA, ROWS), 1)
    pick = jnp.zeros((EXTRA, ROWS), jnp.float32)
    offset = jnp.zeros((EXTRA, 1), jnp.int32)
    for j in range(MEM_ROWS):
        pos = pos_ref[j]
        pick = jnp.where((row == j) & (col == pos % ROWS), 1.0, pick)
        offset = jnp.where(row[:, :1] == MEM_ROWS + j, pos % STRIDE, offset)
    pick = pick.astype(jnp.bfloat16)
    offset = offset.astype(jnp.float32)
    for g in range(N_Z):
        q = q_ref[:, g * GROUP_COLS : (g + 1) * GROUP_COLS]
        o_ref[g, :ROWS] = q
        o_ref[g, ROWS:] = (mix(pick, q) + offset).astype(jnp.bfloat16)


def pack_q(mem_pos, queries):
    return pl.pallas_call(
        pack_q_kernel,
        in_specs=[
            pl.BlockSpec(memory_space=pltpu.SMEM),
            pl.BlockSpec(memory_space=pltpu.VMEM),
        ],
        out_shape=jax.ShapeDtypeStruct((N_Z, ROWS + EXTRA, GROUP_COLS), queries.dtype),
        compiler_params=pltpu.CompilerParams(vmem_limit_bytes=VMEM_LIMIT),
        cost_estimate=pl.CostEstimate(flops=2**27, bytes_accessed=2**21, transcendentals=0),
    )(mem_pos, queries)


def first_kernel(absent_ref, q_ref, *refs):
    pieces, (k_all, v_all, o_ref) = refs[: PRIOR + 1], refs[PRIOR + 1 :]
    for slot, piece in enumerate(pieces):
        for z in range(N_Z):
            at = pl.ds(slot * SPAN + z * ROWS, ROWS)
            k_all[at, :] = piece[z, 0]
            v_all[at, :HEAD_DIM] = piece[z, 1]
            v_all[at, HEAD_DIM:] = jnp.ones((ROWS, HEAD_DIM), jnp.bfloat16)
    absent = absent_ref[0]
    for slot in range(PRIOR):

        @pl.when(slot < absent)
        def _():
            first = k_all[pl.ds(pl.multiple_of(absent * SPAN, SPAN), 16), :][:1, :]
            at = pl.ds(slot * SPAN, SPAN)
            k_all[at, :] = jnp.broadcast_to(first, (SPAN, HEAD_DIM))
            v_all[at, :] = jnp.zeros((SPAN, 2 * HEAD_DIM), jnp.bfloat16)

    extra = [q_ref[z, ROWS:].astype(jnp.float32) for z in range(N_Z)]
    q = jnp.concatenate(
        [
            extra[z][:MEM_ROWS, h * HEAD_DIM : (h + 1) * HEAD_DIM]
            for h in range(GROUP_HEADS)
            for z in range(N_Z)
        ]
    ).astype(jnp.bfloat16)
    offset = jnp.concatenate([extra[z][MEM_ROWS:, :HEAD_DIM] for z in range(N_Z)])[:, :1]
    place = STRIDE * lax.broadcasted_iota(jnp.int32, (SPAN_MEM, 1), 0) + offset.astype(jnp.int32)
    place = jnp.concatenate([place] * GROUP_HEADS)
    count = GROUP_HEADS * SPAN_MEM
    peak = jnp.full((count, 1), -jnp.inf, jnp.float32)
    total = jnp.zeros((count, 2 * HEAD_DIM), jnp.float32)
    for start in (*range(WINDOW, REACH, CHUNK), *range(0, WINDOW, CHUNK)):
        s = scores_of(q, k_all[start : start + CHUNK, :])
        key = start + lax.broadcasted_iota(jnp.int32, (1, CHUNK), 1)
        if start >= WINDOW:
            s = jnp.where(key - WINDOW <= place, s, -jnp.inf)
        if start < SPAN:
            s = jnp.where(key > place, s, -jnp.inf)
        higher = jnp.maximum(peak, jnp.max(s, axis=1, keepdims=True))
        fade = jnp.exp2(peak * COEF - higher * COEF)
        p = jnp.exp2(s * COEF - higher * COEF).astype(jnp.bfloat16)
        total = total * fade + mix(p, v_all[start : start + CHUNK, :])
        peak = higher
    out = (total[:, :HEAD_DIM] / total[:, HEAD_DIM:]).astype(jnp.bfloat16)
    for z in range(N_Z):
        for h in range(GROUP_HEADS):
            o_ref[z, :, h * HEAD_DIM : (h + 1) * HEAD_DIM] = out[
                h * SPAN_MEM : (h + 1) * SPAN_MEM, :
            ]


def attend_first(q, pieces, absent):
    return pl.pallas_call(
        first_kernel,
        in_specs=[pl.BlockSpec(memory_space=pltpu.SMEM)]
        + [pl.BlockSpec(memory_space=pltpu.VMEM)] * (PRIOR + 2),
        out_shape=(
            jax.ShapeDtypeStruct((REACH, HEAD_DIM), q.dtype),
            jax.ShapeDtypeStruct((REACH, 2 * HEAD_DIM), q.dtype),
            jax.ShapeDtypeStruct((N_Z, SPAN_MEM, GROUP_COLS), q.dtype),
        ),
        compiler_params=pltpu.CompilerParams(vmem_limit_bytes=FIRST_LIMIT),
        cost_estimate=pl.CostEstimate(
            flops=GROUP_HEADS * SPAN_MEM * REACH * HEAD_DIM * 8,
            bytes_accessed=8 * 2**20,
            transcendentals=GROUP_HEADS * SPAN_MEM * REACH,
        ),
    )(absent, q, *pieces)


def attend_kernel(heads, q_ref, k_all, v_all, o_ref, q_rows):
    step = pl.program_id(0)
    blocks = TILE // ROWS
    count = heads * TILE
    for h in range(heads):
        for b in range(blocks):
            q_rows[h * TILE + b * ROWS : h * TILE + (b + 1) * ROWS, :] = q_ref[
                b, :ROWS, h * HEAD_DIM : (h + 1) * HEAD_DIM
            ]
    q = q_rows[...]
    start = step * TILE

    def window(ref, offset, size):
        return ref[pl.ds(pl.multiple_of(start + offset, TILE), size), :]

    row = lax.broadcasted_iota(jnp.int32, (1, TILE, TILE), 1)
    col = lax.broadcasted_iota(jnp.int32, (1, TILE, TILE), 2)
    own = col <= row
    oldest = scores_of(q, window(k_all, 0, TILE)).reshape(heads, TILE, TILE)
    newest = scores_of(q, window(k_all, WINDOW, TILE)).reshape(heads, TILE, TILE)
    s = jnp.where(own, newest, oldest).reshape(count, TILE)
    peak = jnp.max(s, axis=1, keepdims=True)
    p = jnp.exp2(s * COEF - peak * COEF).astype(jnp.bfloat16).reshape(heads, TILE, TILE)
    zero = jnp.zeros((), jnp.bfloat16)
    total = mix(jnp.where(own, p, zero).reshape(count, TILE), window(v_all, WINDOW, TILE))
    total += mix(jnp.where(own, zero, p).reshape(count, TILE), window(v_all, 0, TILE))
    offset = TILE
    while offset < WINDOW:
        size = min(CHUNK, WINDOW - offset)
        s = scores_of(q, window(k_all, offset, size))
        higher = jnp.maximum(peak, jnp.max(s, axis=1, keepdims=True))
        fade = jnp.exp2(peak * COEF - higher * COEF)
        p = jnp.exp2(s * COEF - higher * COEF).astype(jnp.bfloat16)
        total = total * fade + mix(p, window(v_all, offset, size))
        peak = higher
        offset += size
    out = (total[:, :HEAD_DIM] / total[:, HEAD_DIM:]).astype(jnp.bfloat16)
    for h in range(heads):
        for b in range(blocks):
            o_ref[b, :, h * HEAD_DIM : (h + 1) * HEAD_DIM] = out[
                h * TILE + b * ROWS : h * TILE + (b + 1) * ROWS, :
            ]


def attend(q, k_all, v_all, part):
    heads = GROUP_HEADS // CALLS
    cols = heads * HEAD_DIM
    blocks = TILE // ROWS
    return pl.pallas_call(
        functools.partial(attend_kernel, heads),
        grid=(SPAN // TILE,),
        in_specs=[
            pl.BlockSpec((blocks, ROWS + EXTRA, cols), lambda i: (i, 0, part)),
            pl.BlockSpec((REACH, HEAD_DIM), lambda i: (0, 0)),
            pl.BlockSpec((REACH, 2 * HEAD_DIM), lambda i: (0, 0)),
        ],
        out_specs=pl.BlockSpec((blocks, ROWS, cols), lambda i: (i, 0, 0)),
        scratch_shapes=[pltpu.VMEM((heads * TILE, HEAD_DIM), jnp.bfloat16)],
        out_shape=jax.ShapeDtypeStruct((N_Z, ROWS, cols), q.dtype),
        compiler_params=pltpu.CompilerParams(vmem_limit_bytes=VMEM_LIMIT),
        cost_estimate=pl.CostEstimate(
            flops=heads * SPAN * WINDOW * HEAD_DIM * 8,
            bytes_accessed=4 * 2**20,
            transcendentals=heads * SPAN * WINDOW,
        ),
    )(q, k_all, v_all)


def unpack_kernel(*refs):
    parts, o_ref = refs[:-1], refs[-1]
    cols = GROUP_COLS // len(parts)
    for g in range(N_Z):
        for c, part in enumerate(parts):
            at = g * GROUP_COLS + c * cols
            o_ref[:, at : at + cols] = part[g]


def unpack(parts):
    return pl.pallas_call(
        unpack_kernel,
        out_shape=jax.ShapeDtypeStruct((ROWS, D), parts[0].dtype),
        compiler_params=pltpu.CompilerParams(vmem_limit_bytes=VMEM_LIMIT),
        cost_estimate=pl.CostEstimate(flops=0, bytes_accessed=2**21, transcendentals=0),
    )(*parts)


def summary_kernel(place_ref, *refs):
    rows, gain_ref, weights = refs[:N_Y], refs[N_Y], refs[N_Y + 1 : N_Y + 5]
    o_ref, normed = refs[N_Y + 5 :]
    y, xl, core = place_ref[0], place_ref[1], place_ref[2]
    for back, rows_ref in enumerate(rows):
        squares = jnp.zeros((SPAN_MEM, 1), jnp.float32)
        for z in range(N_Z):
            picked = rows_ref[z].astype(jnp.float32)
            squares += jnp.sum(picked * picked, axis=1, keepdims=True)
        factor = lax.rsqrt(squares / D + 1e-05)
        at = pl.ds(pl.multiple_of((y - back + N_Y) % N_Y * SPAN_MEM, SPAN_MEM), SPAN_MEM)
        for z in range(N_Z):
            gain = gain_ref[:, z * GROUP_COLS : (z + 1) * GROUP_COLS]
            picked = rows_ref[z].astype(jnp.float32)
            normed[z, at, :] = (picked * factor * gain).astype(jnp.bfloat16)
    total = jnp.zeros(o_ref.shape, jnp.float32)
    half = N_Z // 4
    for i, w_ref in enumerate(weights):
        tp = (xl + i // 2) % 2 * 2 + (core + i % 2) % 2
        for k in range(half):
            cols = slice(k * GROUP_COLS, (k + 1) * GROUP_COLS)
            total += scores_of(w_ref[:, cols], normed[tp * half + k])
    o_ref[...] = total.astype(jnp.bfloat16)


def summarize(place, rows, gain, weights):
    cols = weights[0].shape[0]
    vmem = pl.BlockSpec(memory_space=pltpu.VMEM)
    return pl.pallas_call(
        summary_kernel,
        in_specs=[pl.BlockSpec(memory_space=pltpu.SMEM)] + [vmem] * (N_Y + 5),
        scratch_shapes=[pltpu.VMEM((N_Z, N_Y * SPAN_MEM, GROUP_COLS), jnp.bfloat16)],
        out_shape=jax.ShapeDtypeStruct((cols, N_Y * SPAN_MEM), jnp.bfloat16),
        compiler_params=pltpu.CompilerParams(vmem_limit_bytes=VMEM_LIMIT),
        cost_estimate=pl.CostEstimate(
            flops=2 * N_Y * SPAN_MEM * D * cols,
            bytes_accessed=4 * 2**20,
            transcendentals=0,
        ),
    )(place, *rows, gain.reshape(1, D), *weights)


def together(*values):
    return lax.optimization_barrier(values)


def exchange(a, axis):
    return lax.all_to_all(a, axis, split_axis=0, concat_axis=0, tiled=True)


def from_group_behind(a, back):
    def index(group):
        return group % N_Y * (GROUPS // N_Y) + group // N_Y

    return lax.ppermute(a, PLACES, [(index(g - back), index(g)) for g in range(back, GROUPS)])


def on_device(queries, keys, values, mem_pos, norm_gain, summary_weight):
    xl, core, y = lax.axis_index("xl"), lax.axis_index("core"), lax.axis_index("y")
    place = (xl * 2 + core) * N_Y + y
    absent = jnp.maximum(PRIOR - place, 0).astype(jnp.int32).reshape(1)

    kv = pack_kv(keys, values)
    own = exchange(kv, "z")
    weight, _ = together(summary_weight.T, kv)
    across = lax.ppermute(weight, "xl", SWAP)
    beside = lax.ppermute(weight, "core", SWAP)
    weights = [weight, beside, across, lax.ppermute(across, "core", SWAP)]
    own, q, weights = together(own, pack_q(mem_pos, queries), weights)
    q = exchange(q, "z")
    pieces = [from_group_behind(own, back) for back in range(PRIOR, 0, -1)] + [own]
    k_all, v_all, picked = attend_first(q, pieces, absent)

    picked = exchange(picked, "z")
    out, picked = together(attend(q, k_all, v_all, 0), picked)
    rows = [picked] + [
        lax.ppermute(picked, "y", [(i, (i + back) % N_Y) for i in range(N_Y)])
        for back in range(1, N_Y)
    ]
    sent = [exchange(out, "z")]
    for part in range(1, CALLS):
        out, sent = together(attend(q, k_all, v_all, part), sent)
        if part == CALLS - 1:
            out, rows[1], rows[3] = together(out, rows[1], rows[3])
        sent = sent + [exchange(out, "z")]
    summary = summarize(jnp.stack((y, xl, core)), rows, norm_gain, weights)
    sent, summary = together(sent, summary)
    return unpack(sent), summary.T


def solution(mesh):
    split = Mesh(mesh.devices.reshape(-1, N_Y, N_Z, 2, 2), ("file", "y", "z", "xl", "core"))
    tokens = ("file", "xl", "core", "y", "z")
    return jax.shard_map(
        on_device,
        mesh=split,
        in_specs=(
            P(tokens, None),
            P(tokens, None),
            P(tokens, None),
            P(tokens),
            P(),
            P(("xl", "core"), ("y", "z")),
        ),
        out_specs=(P(tokens, None), P(("file", "xl", "core"), ("y", "z"))),
        check_vma=False,
    )
```

```python
import functools

import jax
import jax.numpy as jnp
from jax import lax
from jax.experimental import pallas as pl
from jax.experimental.pallas import tpu as pltpu
from jax.sharding import Mesh, PartitionSpec as P

D = 4096
HEADS = 32
KV_HEADS = 8
HEAD_DIM = 128
GROUP_HEADS = HEADS // KV_HEADS
GROUP_COLS = GROUP_HEADS * HEAD_DIM
ROWS = 128
MEM_ROWS = 8
STRIDE = ROWS // MEM_ROWS
EXTRA = 16
N_Z = 8
N_Y = 4
SPAN = ROWS * N_Z
SPAN_MEM = MEM_ROWS * N_Z
WINDOW = 4096
REACH = WINDOW + SPAN
PRIOR = WINDOW // SPAN
TILE = 256
CHUNK = 512
CALLS = 2
COEF = 1.4426950408889634 / HEAD_DIM**0.5
VMEM_LIMIT = 14 * 2**20
PACK_LIMIT = 60 * 2**20
PLACES = ("y", "xl", "core")
GROUPS = 4 * N_Y
SWAP = [(0, 1), (1, 0)]
LAID_OUT = [
    pltpu.VMEM((REACH, 2 * HEAD_DIM), jnp.bfloat16),
    pltpu.VMEM((REACH, 2 * HEAD_DIM), jnp.bfloat16),
]


def scores_of(q, k):
    return lax.dot_general(q, k, (((1,), (1,)), ((), ())), preferred_element_type=jnp.float32)


def mix(p, v):
    return jnp.dot(p, v, preferred_element_type=jnp.float32)


def pack_kv_kernel(k_ref, v_ref, o_ref):
    for g in range(KV_HEADS):
        cols = slice(g * HEAD_DIM, (g + 1) * HEAD_DIM)
        o_ref[g, 0] = k_ref[:, cols]
        o_ref[g, 1] = v_ref[:, cols]


def pack_kv(keys, values):
    return pl.pallas_call(
        pack_kv_kernel,
        out_shape=jax.ShapeDtypeStruct((KV_HEADS, 2, ROWS, HEAD_DIM), keys.dtype),
        compiler_params=pltpu.CompilerParams(vmem_limit_bytes=PACK_LIMIT),
        cost_estimate=pl.CostEstimate(flops=0, bytes_accessed=2**20, transcendentals=0),
    )(keys, values)


def pack_q_kernel(pos_ref, q_ref, o_ref):
    row = lax.broadcasted_iota(jnp.int32, (EXTRA, ROWS), 0)
    col = lax.broadcasted_iota(jnp.int32, (EXTRA, ROWS), 1)
    pick = jnp.zeros((EXTRA, ROWS), jnp.float32)
    offset = jnp.zeros((EXTRA, 1), jnp.int32)
    for j in range(MEM_ROWS):
        pos = pos_ref[j]
        pick = jnp.where((row == j) & (col == pos % ROWS), 1.0, pick)
        offset = jnp.where(row[:, :1] == MEM_ROWS + j, pos % STRIDE, offset)
    pick = pick.astype(jnp.bfloat16)
    offset = offset.astype(jnp.float32)
    for g in range(N_Z):
        q = q_ref[:, g * GROUP_COLS : (g + 1) * GROUP_COLS]
        o_ref[g, :ROWS] = q
        o_ref[g, ROWS:] = (mix(pick, q) + offset).astype(jnp.bfloat16)


def pack_q(mem_pos, queries):
    return pl.pallas_call(
        pack_q_kernel,
        in_specs=[
            pl.BlockSpec(memory_space=pltpu.SMEM),
            pl.BlockSpec(memory_space=pltpu.VMEM),
        ],
        out_shape=jax.ShapeDtypeStruct((N_Z, ROWS + EXTRA, GROUP_COLS), queries.dtype),
        compiler_params=pltpu.CompilerParams(vmem_limit_bytes=VMEM_LIMIT),
        cost_estimate=pl.CostEstimate(flops=2**27, bytes_accessed=2**21, transcendentals=0),
    )(mem_pos, queries)


def lay_out(absent_ref, pieces, k_all, v_all):
    for slot, piece in enumerate(pieces):
        for z in range(N_Z):
            at = pl.ds(slot * SPAN + z * ROWS, ROWS)
            k_all[at, :HEAD_DIM] = piece[z, 0]
            k_all[at, HEAD_DIM:] = piece[z, 0]
            v_all[at, :HEAD_DIM] = piece[z, 1]
            v_all[at, HEAD_DIM:] = jnp.ones((ROWS, HEAD_DIM), jnp.bfloat16)
    absent = absent_ref[0]
    for slot in range(PRIOR):

        @pl.when(slot < absent)
        def _():
            first = k_all[pl.ds(pl.multiple_of(absent * SPAN, SPAN), 16), :][:1, :]
            at = pl.ds(slot * SPAN, SPAN)
            k_all[at, :] = jnp.broadcast_to(first, (SPAN, 2 * HEAD_DIM))
            v_all[at, :] = jnp.zeros((SPAN, 2 * HEAD_DIM), jnp.bfloat16)


def first_kernel(absent_ref, q_ref, *refs):
    pieces, (o_ref, k_all, v_all) = refs[: PRIOR + 1], refs[PRIOR + 1 :]
    lay_out(absent_ref, pieces, k_all, v_all)
    extra = [q_ref[z, ROWS:].astype(jnp.float32) for z in range(N_Z)]
    q = jnp.concatenate(
        [
            extra[z][:MEM_ROWS, h * HEAD_DIM : (h + 1) * HEAD_DIM]
            for h in range(GROUP_HEADS)
            for z in range(N_Z)
        ]
    ).astype(jnp.bfloat16)
    offset = jnp.concatenate([extra[z][MEM_ROWS:, :HEAD_DIM] for z in range(N_Z)])[:, :1]
    place = STRIDE * lax.broadcasted_iota(jnp.int32, (SPAN_MEM, 1), 0) + offset.astype(jnp.int32)
    place = jnp.concatenate([place] * GROUP_HEADS)
    count = GROUP_HEADS * SPAN_MEM
    peak = jnp.full((count, 1), -jnp.inf, jnp.float32)
    total = jnp.zeros((count, 2 * HEAD_DIM), jnp.float32)
    for start in (*range(WINDOW, REACH, CHUNK), *range(0, WINDOW, CHUNK)):
        s = scores_of(q, k_all[start : start + CHUNK, :HEAD_DIM])
        key = start + lax.broadcasted_iota(jnp.int32, (1, CHUNK), 1)
        if start >= WINDOW:
            s = jnp.where(key - WINDOW <= place, s, -jnp.inf)
        if start < SPAN:
            s = jnp.where(key > place, s, -jnp.inf)
        higher = jnp.maximum(peak, jnp.max(s, axis=1, keepdims=True))
        fade = jnp.exp2(peak * COEF - higher * COEF)
        p = jnp.exp2(s * COEF - higher * COEF).astype(jnp.bfloat16)
        total = total * fade + mix(p, v_all[start : start + CHUNK, :])
        peak = higher
    out = (total[:, :HEAD_DIM] / total[:, HEAD_DIM:]).astype(jnp.bfloat16)
    for z in range(N_Z):
        for h in range(GROUP_HEADS):
            o_ref[z, :, h * HEAD_DIM : (h + 1) * HEAD_DIM] = out[
                h * SPAN_MEM : (h + 1) * SPAN_MEM, :
            ]


def attend_first(q, pieces, absent):
    return pl.pallas_call(
        first_kernel,
        in_specs=[pl.BlockSpec(memory_space=pltpu.SMEM)]
        + [pl.BlockSpec(memory_space=pltpu.VMEM)] * (PRIOR + 2),
        scratch_shapes=LAID_OUT,
        out_shape=jax.ShapeDtypeStruct((N_Z, SPAN_MEM, GROUP_COLS), q.dtype),
        compiler_params=pltpu.CompilerParams(vmem_limit_bytes=VMEM_LIMIT),
        cost_estimate=pl.CostEstimate(
            flops=GROUP_HEADS * SPAN_MEM * REACH * HEAD_DIM * 8,
            bytes_accessed=8 * 2**20,
            transcendentals=GROUP_HEADS * SPAN_MEM * REACH,
        ),
    )(absent, q, *pieces)


def attend_kernel(heads, absent_ref, q_ref, *refs):
    pieces, (o_ref, k_all, v_all, q_rows) = refs[: PRIOR + 1], refs[PRIOR + 1 :]
    step = pl.program_id(0)

    @pl.when(step == 0)
    def _():
        lay_out(absent_ref, pieces, k_all, v_all)

    blocks = TILE // ROWS
    count = heads * TILE
    for h in range(heads):
        for b in range(blocks):
            at = slice(h * TILE + b * ROWS, h * TILE + (b + 1) * ROWS)
            scaled = q_ref[b, :ROWS, h * HEAD_DIM : (h + 1) * HEAD_DIM].astype(jnp.float32) * COEF
            leading = scaled.astype(jnp.bfloat16)
            q_rows[at, :HEAD_DIM] = leading
            q_rows[at, HEAD_DIM:] = (scaled - leading.astype(jnp.float32)).astype(jnp.bfloat16)
    q = q_rows[...]
    start = step * TILE

    def window(ref, offset, size):
        return ref[pl.ds(pl.multiple_of(start + offset, TILE), size), :]

    row = lax.broadcasted_iota(jnp.int32, (1, TILE, TILE), 1)
    col = lax.broadcasted_iota(jnp.int32, (1, TILE, TILE), 2)
    own = col <= row
    oldest = scores_of(q, window(k_all, 0, TILE)).reshape(heads, TILE, TILE)
    newest = scores_of(q, window(k_all, WINDOW, TILE)).reshape(heads, TILE, TILE)
    s = jnp.where(own, newest, oldest).reshape(count, TILE)
    peak = jnp.max(s, axis=1, keepdims=True)
    p = jnp.exp2(s - peak).astype(jnp.bfloat16).reshape(heads, TILE, TILE)
    zero = jnp.zeros((), jnp.bfloat16)
    total = mix(jnp.where(own, p, zero).reshape(count, TILE), window(v_all, WINDOW, TILE))
    total += mix(jnp.where(own, zero, p).reshape(count, TILE), window(v_all, 0, TILE))
    offset = TILE
    while offset < WINDOW:
        size = min(CHUNK, WINDOW - offset)
        s = scores_of(q, window(k_all, offset, size))
        higher = jnp.maximum(peak, jnp.max(s, axis=1, keepdims=True))
        fade = jnp.exp2(peak - higher)
        p = jnp.exp2(s - higher).astype(jnp.bfloat16)
        total = total * fade + mix(p, window(v_all, offset, size))
        peak = higher
        offset += size
    out = (total[:, :HEAD_DIM] / total[:, HEAD_DIM:]).astype(jnp.bfloat16)
    for h in range(heads):
        for b in range(blocks):
            o_ref[b, :, h * HEAD_DIM : (h + 1) * HEAD_DIM] = out[
                h * TILE + b * ROWS : h * TILE + (b + 1) * ROWS, :
            ]


def attend(q, pieces, absent, part):
    heads = GROUP_HEADS // CALLS
    cols = heads * HEAD_DIM
    blocks = TILE // ROWS
    return pl.pallas_call(
        functools.partial(attend_kernel, heads),
        grid=(SPAN // TILE,),
        in_specs=[
            pl.BlockSpec(memory_space=pltpu.SMEM),
            pl.BlockSpec((blocks, ROWS + EXTRA, cols), lambda i: (i, 0, part)),
        ]
        + [pl.BlockSpec(memory_space=pltpu.VMEM)] * (PRIOR + 1),
        out_specs=pl.BlockSpec((blocks, ROWS, cols), lambda i: (i, 0, 0)),
        scratch_shapes=LAID_OUT + [pltpu.VMEM((heads * TILE, 2 * HEAD_DIM), jnp.bfloat16)],
        out_shape=jax.ShapeDtypeStruct((N_Z, ROWS, cols), q.dtype),
        compiler_params=pltpu.CompilerParams(vmem_limit_bytes=VMEM_LIMIT),
        cost_estimate=pl.CostEstimate(
            flops=heads * SPAN * WINDOW * HEAD_DIM * 8,
            bytes_accessed=4 * 2**20,
            transcendentals=heads * SPAN * WINDOW,
        ),
    )(absent, q, *pieces)


def unpack_kernel(*refs):
    parts, o_ref = refs[:-1], refs[-1]
    cols = GROUP_COLS // len(parts)
    for g in range(N_Z):
        for c, part in enumerate(parts):
            at = g * GROUP_COLS + c * cols
            o_ref[:, at : at + cols] = part[g]


def unpack(parts):
    return pl.pallas_call(
        unpack_kernel,
        out_shape=jax.ShapeDtypeStruct((ROWS, D), parts[0].dtype),
        compiler_params=pltpu.CompilerParams(vmem_limit_bytes=VMEM_LIMIT),
        cost_estimate=pl.CostEstimate(flops=0, bytes_accessed=2**21, transcendentals=0),
    )(*parts)


def summary_kernel(place_ref, *refs):
    rows, gain_ref, weights = refs[: N_Y + 1], refs[N_Y + 1], refs[N_Y + 2 : N_Y + 6]
    o_ref, normed = refs[N_Y + 6 :]
    blocks = [[rows[0]], [rows[1]], rows[2:4], [rows[4]]]
    y, xl, core = place_ref[0], place_ref[1], place_ref[2]
    for back, block in enumerate(blocks):
        block = [ref[z] for ref in block for z in range(ref.shape[0])]
        squares = jnp.zeros((SPAN_MEM, 1), jnp.float32)
        for z in range(N_Z):
            picked = block[z].astype(jnp.float32)
            squares += jnp.sum(picked * picked, axis=1, keepdims=True)
        factor = lax.rsqrt(squares / D + 1e-05)
        at = pl.ds(pl.multiple_of((y - back + N_Y) % N_Y * SPAN_MEM, SPAN_MEM), SPAN_MEM)
        for z in range(N_Z):
            gain = gain_ref[:, z * GROUP_COLS : (z + 1) * GROUP_COLS]
            picked = block[z].astype(jnp.float32)
            normed[z, at, :] = (picked * factor * gain).astype(jnp.bfloat16)
    total = jnp.zeros(o_ref.shape, jnp.float32)
    per = N_Z // 4
    for i, w_ref in enumerate(weights):
        tp = (xl + i // 2) % 2 * 2 + (core + i % 2) % 2
        for k in range(per):
            cols = slice(k * GROUP_COLS, (k + 1) * GROUP_COLS)
            total += scores_of(w_ref[:, cols], normed[tp * per + k])
    o_ref[...] = total.astype(jnp.bfloat16)


def summarize(place, rows, gain, weights):
    cols = weights[0].shape[0]
    vmem = pl.BlockSpec(memory_space=pltpu.VMEM)
    return pl.pallas_call(
        summary_kernel,
        in_specs=[pl.BlockSpec(memory_space=pltpu.SMEM)] + [vmem] * (N_Y + 6),
        scratch_shapes=[pltpu.VMEM((N_Z, N_Y * SPAN_MEM, GROUP_COLS), jnp.bfloat16)],
        out_shape=jax.ShapeDtypeStruct((cols, N_Y * SPAN_MEM), jnp.bfloat16),
        compiler_params=pltpu.CompilerParams(vmem_limit_bytes=VMEM_LIMIT),
        cost_estimate=pl.CostEstimate(
            flops=2 * N_Y * SPAN_MEM * D * cols,
            bytes_accessed=4 * 2**20,
            transcendentals=0,
        ),
    )(place, *rows, gain.reshape(1, D), *weights)


def together(*values):
    return lax.optimization_barrier(values)


def exchange(a, axis):
    return lax.all_to_all(a, axis, split_axis=0, concat_axis=0, tiled=True)


def from_group_behind(a, back):
    def index(group):
        return group % N_Y * (GROUPS // N_Y) + group // N_Y

    return lax.ppermute(a, PLACES, [(index(g - back), index(g)) for g in range(back, GROUPS)])


def on_device(queries, keys, values, mem_pos, norm_gain, summary_weight):
    xl, core, y = lax.axis_index("xl"), lax.axis_index("core"), lax.axis_index("y")
    place = (xl * 2 + core) * N_Y + y
    absent = jnp.maximum(PRIOR - place, 0).astype(jnp.int32).reshape(1)

    kv = pack_kv(keys, values)
    own = exchange(kv, "z")
    weight, _ = together(summary_weight.T, kv)
    across = lax.ppermute(weight, "xl", SWAP)
    beside = lax.ppermute(weight, "core", SWAP)
    own, q, across, beside = together(own, pack_q(mem_pos, queries), across, beside)
    weights = [weight, beside, across, lax.ppermute(across, "core", SWAP)]
    q = exchange(q, "z")
    pieces = [from_group_behind(own, back) for back in range(PRIOR, 0, -1)] + [own]
    q, weights = together(q, weights)
    picked = attend_first(q, pieces, absent)

    picked = exchange(picked, "z")
    out, picked = together(attend(q, pieces, absent, 0), picked)
    def from_y_behind(a, back):
        return lax.ppermute(a, "y", [(i, (i + back) % N_Y) for i in range(N_Y)])

    low = picked[: N_Z // 2]
    next_to = [from_y_behind(picked, 1), from_y_behind(picked, 3), from_y_behind(low, 2)]
    sent = [exchange(out, "z")]
    for part in range(1, CALLS):
        out, sent = together(attend(q, pieces, absent, part), sent)
        if part == CALLS - 1:
            out, next_to, picked = together(out, next_to, picked)
        sent = sent + [exchange(out, "z")]
    high = picked[N_Z // 2 :]
    rows = [picked, next_to[0], next_to[2], from_y_behind(high, 2), next_to[1]]
    summary = summarize(jnp.stack((y, xl, core)), rows, norm_gain, weights)
    sent, summary = together(sent, summary)
    return unpack(sent), summary.T


def solution(mesh):
    split = Mesh(mesh.devices.reshape(-1, N_Y, N_Z, 2, 2), ("file", "y", "z", "xl", "core"))
    tokens = ("file", "xl", "core", "y", "z")
    return jax.shard_map(
        on_device,
        mesh=split,
        in_specs=(
            P(tokens, None),
            P(tokens, None),
            P(tokens, None),
            P(tokens),
            P(),
            P(("xl", "core"), ("y", "z")),
        ),
        out_specs=(P(tokens, None), P(("file", "xl", "core"), ("y", "z"))),
        check_vma=False,
    )
```

```python
import functools

import jax
import jax.numpy as jnp
from jax import lax
from jax.experimental import pallas as pl
from jax.experimental.pallas import tpu as pltpu
from jax.sharding import Mesh, PartitionSpec as P

D = 4096
HEADS = 32
KV_HEADS = 8
HEAD_DIM = 128
GROUP_HEADS = HEADS // KV_HEADS
GROUP_COLS = GROUP_HEADS * HEAD_DIM
ROWS = 128
MEM_ROWS = 8
STRIDE = ROWS // MEM_ROWS
EXTRA = 16
N_Z = 8
N_Y = 4
SPAN = ROWS * N_Z
SPAN_MEM = MEM_ROWS * N_Z
WINDOW = 4096
REACH = WINDOW + SPAN
PRIOR = WINDOW // SPAN
TILE = 256
CHUNK = 512
CALLS = 2
COEF = 1.4426950408889634 / HEAD_DIM**0.5
VMEM_LIMIT = 14 * 2**20
PACK_LIMIT = 60 * 2**20
PLACES = ("y", "xl", "core")
GROUPS = 4 * N_Y
SWAP = [(0, 1), (1, 0)]
SLOTS = (0, 2, 1, 3)
LAID_OUT = [
    pltpu.VMEM((REACH, 2 * HEAD_DIM), jnp.bfloat16),
    pltpu.VMEM((REACH, 2 * HEAD_DIM), jnp.bfloat16),
]


def scores_of(q, k):
    return lax.dot_general(q, k, (((1,), (1,)), ((), ())), preferred_element_type=jnp.float32)


def mix(p, v):
    return jnp.dot(p, v, preferred_element_type=jnp.float32)


def pack_kv_kernel(k_ref, v_ref, o_ref):
    for g in range(KV_HEADS):
        cols = slice(g * HEAD_DIM, (g + 1) * HEAD_DIM)
        o_ref[g, 0] = k_ref[:, cols]
        o_ref[g, 1] = v_ref[:, cols]


def pack_kv(keys, values):
    return pl.pallas_call(
        pack_kv_kernel,
        out_shape=jax.ShapeDtypeStruct((KV_HEADS, 2, ROWS, HEAD_DIM), keys.dtype),
        compiler_params=pltpu.CompilerParams(vmem_limit_bytes=PACK_LIMIT),
        cost_estimate=pl.CostEstimate(flops=0, bytes_accessed=2**20, transcendentals=0),
    )(keys, values)


def pack_q_kernel(pos_ref, q_ref, o_ref):
    row = lax.broadcasted_iota(jnp.int32, (EXTRA, ROWS), 0)
    col = lax.broadcasted_iota(jnp.int32, (EXTRA, ROWS), 1)
    pick = jnp.zeros((EXTRA, ROWS), jnp.float32)
    offset = jnp.zeros((EXTRA, 1), jnp.int32)
    for j in range(MEM_ROWS):
        pos = pos_ref[j]
        pick = jnp.where((row == j) & (col == pos % ROWS), 1.0, pick)
        offset = jnp.where(row[:, :1] == MEM_ROWS + j, pos % STRIDE, offset)
    pick = pick.astype(jnp.bfloat16)
    offset = offset.astype(jnp.float32)
    for g in range(N_Z):
        q = q_ref[:, g * GROUP_COLS : (g + 1) * GROUP_COLS]
        o_ref[g, :ROWS] = q
        o_ref[g, ROWS:] = (mix(pick, q) + offset).astype(jnp.bfloat16)


def pack_q(mem_pos, queries):
    return pl.pallas_call(
        pack_q_kernel,
        in_specs=[
            pl.BlockSpec(memory_space=pltpu.SMEM),
            pl.BlockSpec(memory_space=pltpu.VMEM),
        ],
        out_shape=jax.ShapeDtypeStruct((N_Z, ROWS + EXTRA, GROUP_COLS), queries.dtype),
        compiler_params=pltpu.CompilerParams(vmem_limit_bytes=VMEM_LIMIT),
        cost_estimate=pl.CostEstimate(flops=2**27, bytes_accessed=2**21, transcendentals=0),
    )(mem_pos, queries)


def lay_out(absent_ref, pieces, k_all, v_all):
    for slot, piece in zip((*SLOTS, PRIOR), pieces):
        for z in range(N_Z):
            at = pl.ds(slot * SPAN + z * ROWS, ROWS)
            k_all[at, :HEAD_DIM] = piece[z, 0]
            k_all[at, HEAD_DIM:] = piece[z, 0]
            v_all[at, :HEAD_DIM] = piece[z, 1]
            v_all[at, HEAD_DIM:] = jnp.ones((ROWS, HEAD_DIM), jnp.bfloat16)
    absent = absent_ref[0]
    for slot in range(PRIOR):

        @pl.when(slot < absent)
        def _():
            first = k_all[pl.ds(pl.multiple_of(absent * SPAN, SPAN), 16), :][:1, :]
            at = pl.ds(slot * SPAN, SPAN)
            k_all[at, :] = jnp.broadcast_to(first, (SPAN, 2 * HEAD_DIM))
            v_all[at, :] = jnp.zeros((SPAN, 2 * HEAD_DIM), jnp.bfloat16)


def first_kernel(absent_ref, q_ref, *refs):
    pieces, (o_ref, k_all, v_all) = refs[: PRIOR + 1], refs[PRIOR + 1 :]
    lay_out(absent_ref, pieces, k_all, v_all)
    extra = [q_ref[z, ROWS:].astype(jnp.float32) for z in range(N_Z)]
    q = jnp.concatenate(
        [
            extra[z][:MEM_ROWS, h * HEAD_DIM : (h + 1) * HEAD_DIM]
            for h in range(GROUP_HEADS)
            for z in range(N_Z)
        ]
    ).astype(jnp.bfloat16)
    offset = jnp.concatenate([extra[z][MEM_ROWS:, :HEAD_DIM] for z in range(N_Z)])[:, :1]
    place = STRIDE * lax.broadcasted_iota(jnp.int32, (SPAN_MEM, 1), 0) + offset.astype(jnp.int32)
    place = jnp.concatenate([place] * GROUP_HEADS)
    count = GROUP_HEADS * SPAN_MEM
    peak = jnp.full((count, 1), -jnp.inf, jnp.float32)
    total = jnp.zeros((count, 2 * HEAD_DIM), jnp.float32)
    for start in (*range(WINDOW, REACH, CHUNK), *range(0, WINDOW, CHUNK)):
        s = scores_of(q, k_all[start : start + CHUNK, :HEAD_DIM])
        key = start + lax.broadcasted_iota(jnp.int32, (1, CHUNK), 1)
        if start >= WINDOW:
            s = jnp.where(key - WINDOW <= place, s, -jnp.inf)
        if start < SPAN:
            s = jnp.where(key > place, s, -jnp.inf)
        higher = jnp.maximum(peak, jnp.max(s, axis=1, keepdims=True))
        fade = jnp.exp2(peak * COEF - higher * COEF)
        p = jnp.exp2(s * COEF - higher * COEF).astype(jnp.bfloat16)
        total = total * fade + mix(p, v_all[start : start + CHUNK, :])
        peak = higher
    out = (total[:, :HEAD_DIM] / total[:, HEAD_DIM:]).astype(jnp.bfloat16)
    for z in range(N_Z):
        for h in range(GROUP_HEADS):
            o_ref[z, :, h * HEAD_DIM : (h + 1) * HEAD_DIM] = out[
                h * SPAN_MEM : (h + 1) * SPAN_MEM, :
            ]


def attend_first(q, pieces, absent):
    return pl.pallas_call(
        first_kernel,
        in_specs=[pl.BlockSpec(memory_space=pltpu.SMEM)]
        + [pl.BlockSpec(memory_space=pltpu.VMEM)] * (PRIOR + 2),
        scratch_shapes=LAID_OUT,
        out_shape=jax.ShapeDtypeStruct((N_Z, SPAN_MEM, GROUP_COLS), q.dtype),
        compiler_params=pltpu.CompilerParams(vmem_limit_bytes=VMEM_LIMIT),
        cost_estimate=pl.CostEstimate(
            flops=GROUP_HEADS * SPAN_MEM * REACH * HEAD_DIM * 8,
            bytes_accessed=8 * 2**20,
            transcendentals=GROUP_HEADS * SPAN_MEM * REACH,
        ),
    )(absent, q, *pieces)


def attend_kernel(heads, absent_ref, q_ref, *refs):
    pieces, (o_ref, k_all, v_all, q_rows) = refs[: PRIOR + 1], refs[PRIOR + 1 :]
    step = pl.program_id(0)

    @pl.when(step == 0)
    def _():
        lay_out(absent_ref, pieces, k_all, v_all)

    blocks = TILE // ROWS
    count = heads * TILE
    for h in range(heads):
        for b in range(blocks):
            at = slice(h * TILE + b * ROWS, h * TILE + (b + 1) * ROWS)
            scaled = q_ref[b, :ROWS, h * HEAD_DIM : (h + 1) * HEAD_DIM].astype(jnp.float32) * COEF
            leading = scaled.astype(jnp.bfloat16)
            q_rows[at, :HEAD_DIM] = leading
            q_rows[at, HEAD_DIM:] = (scaled - leading.astype(jnp.float32)).astype(jnp.bfloat16)
    q = q_rows[...]
    start = step * TILE

    def window(ref, offset, size):
        return ref[pl.ds(pl.multiple_of(start + offset, TILE), size), :]

    row = lax.broadcasted_iota(jnp.int32, (1, TILE, TILE), 1)
    col = lax.broadcasted_iota(jnp.int32, (1, TILE, TILE), 2)
    own = col <= row
    oldest = scores_of(q, window(k_all, 0, TILE)).reshape(heads, TILE, TILE)
    newest = scores_of(q, window(k_all, WINDOW, TILE)).reshape(heads, TILE, TILE)
    s = jnp.where(own, newest, oldest).reshape(count, TILE)
    peak = jnp.max(s, axis=1, keepdims=True)
    p = jnp.exp2(s - peak).astype(jnp.bfloat16).reshape(heads, TILE, TILE)
    zero = jnp.zeros((), jnp.bfloat16)
    total = mix(jnp.where(own, p, zero).reshape(count, TILE), window(v_all, WINDOW, TILE))
    total += mix(jnp.where(own, zero, p).reshape(count, TILE), window(v_all, 0, TILE))
    offset = TILE
    while offset < WINDOW:
        size = min(CHUNK, WINDOW - offset)
        s = scores_of(q, window(k_all, offset, size))
        higher = jnp.maximum(peak, jnp.max(s, axis=1, keepdims=True))
        fade = jnp.exp2(peak - higher)
        p = jnp.exp2(s - higher).astype(jnp.bfloat16)
        total = total * fade + mix(p, window(v_all, offset, size))
        peak = higher
        offset += size
    out = (total[:, :HEAD_DIM] / total[:, HEAD_DIM:]).astype(jnp.bfloat16)
    for h in range(heads):
        for b in range(blocks):
            o_ref[b, :, h * HEAD_DIM : (h + 1) * HEAD_DIM] = out[
                h * TILE + b * ROWS : h * TILE + (b + 1) * ROWS, :
            ]


def attend(q, pieces, absent, part):
    heads = GROUP_HEADS // CALLS
    cols = heads * HEAD_DIM
    blocks = TILE // ROWS
    return pl.pallas_call(
        functools.partial(attend_kernel, heads),
        grid=(SPAN // TILE,),
        in_specs=[
            pl.BlockSpec(memory_space=pltpu.SMEM),
            pl.BlockSpec((blocks, ROWS + EXTRA, cols), lambda i: (i, 0, part)),
        ]
        + [pl.BlockSpec(memory_space=pltpu.VMEM)] * (PRIOR + 1),
        out_specs=pl.BlockSpec((blocks, ROWS, cols), lambda i: (i, 0, 0)),
        scratch_shapes=LAID_OUT + [pltpu.VMEM((heads * TILE, 2 * HEAD_DIM), jnp.bfloat16)],
        out_shape=jax.ShapeDtypeStruct((N_Z, ROWS, cols), q.dtype),
        compiler_params=pltpu.CompilerParams(vmem_limit_bytes=VMEM_LIMIT),
        cost_estimate=pl.CostEstimate(
            flops=heads * SPAN * WINDOW * HEAD_DIM * 8,
            bytes_accessed=4 * 2**20,
            transcendentals=heads * SPAN * WINDOW,
        ),
    )(absent, q, *pieces)


def unpack_kernel(*refs):
    parts, o_ref = refs[:-1], refs[-1]
    cols = GROUP_COLS // len(parts)
    for g in range(N_Z):
        for c, part in enumerate(parts):
            at = g * GROUP_COLS + c * cols
            o_ref[:, at : at + cols] = part[g]


def unpack(parts):
    return pl.pallas_call(
        unpack_kernel,
        out_shape=jax.ShapeDtypeStruct((ROWS, D), parts[0].dtype),
        compiler_params=pltpu.CompilerParams(vmem_limit_bytes=VMEM_LIMIT),
        cost_estimate=pl.CostEstimate(flops=0, bytes_accessed=2**21, transcendentals=0),
    )(*parts)


def summary_kernel(place_ref, *refs):
    rows, gain_ref, weights = refs[: N_Y + 1], refs[N_Y + 1], refs[N_Y + 2 : N_Y + 6]
    o_ref, normed = refs[N_Y + 6 :]
    blocks = [[rows[0]], [rows[1]], rows[2:4], [rows[4]]]
    y, xl, core = place_ref[0], place_ref[1], place_ref[2]
    for back, block in enumerate(blocks):
        block = [ref[z] for ref in block for z in range(ref.shape[0])]
        squares = jnp.zeros((SPAN_MEM, 1), jnp.float32)
        for z in range(N_Z):
            picked = block[z].astype(jnp.float32)
            squares += jnp.sum(picked * picked, axis=1, keepdims=True)
        factor = lax.rsqrt(squares / D + 1e-05)
        at = pl.ds(pl.multiple_of((y - back + N_Y) % N_Y * SPAN_MEM, SPAN_MEM), SPAN_MEM)
        for z in range(N_Z):
            gain = gain_ref[:, z * GROUP_COLS : (z + 1) * GROUP_COLS]
            picked = block[z].astype(jnp.float32)
            normed[z, at, :] = (picked * factor * gain).astype(jnp.bfloat16)
    total = jnp.zeros(o_ref.shape, jnp.float32)
    per = N_Z // 4
    for i, w_ref in enumerate(weights):
        tp = (xl + i // 2) % 2 * 2 + (core + i % 2) % 2
        for k in range(per):
            cols = slice(k * GROUP_COLS, (k + 1) * GROUP_COLS)
            total += scores_of(w_ref[:, cols], normed[tp * per + k])
    o_ref[...] = total.astype(jnp.bfloat16)


def summarize(place, rows, gain, weights):
    cols = weights[0].shape[0]
    vmem = pl.BlockSpec(memory_space=pltpu.VMEM)
    return pl.pallas_call(
        summary_kernel,
        in_specs=[pl.BlockSpec(memory_space=pltpu.SMEM)] + [vmem] * (N_Y + 6),
        scratch_shapes=[pltpu.VMEM((N_Z, N_Y * SPAN_MEM, GROUP_COLS), jnp.bfloat16)],
        out_shape=jax.ShapeDtypeStruct((cols, N_Y * SPAN_MEM), jnp.bfloat16),
        compiler_params=pltpu.CompilerParams(vmem_limit_bytes=VMEM_LIMIT),
        cost_estimate=pl.CostEstimate(
            flops=2 * N_Y * SPAN_MEM * D * cols,
            bytes_accessed=4 * 2**20,
            transcendentals=0,
        ),
    )(place, *rows, gain.reshape(1, D), *weights)


def together(*values):
    return lax.optimization_barrier(values)


def exchange(a, axis):
    return lax.all_to_all(a, axis, split_axis=0, concat_axis=0, tiled=True)


def from_group_behind(a, back):
    def index(group):
        return group % N_Y * (GROUPS // N_Y) + group // N_Y

    return lax.ppermute(a, PLACES, [(index(g - back), index(g)) for g in range(back, GROUPS)])


def on_device(queries, keys, values, mem_pos, norm_gain, summary_weight):
    xl, core, y = lax.axis_index("xl"), lax.axis_index("core"), lax.axis_index("y")
    place = (xl * 2 + core) * N_Y + y
    absent = jnp.maximum(PRIOR - place, 0).astype(jnp.int32).reshape(1)

    kv = pack_kv(keys, values)
    own = exchange(kv, "z")
    weight, _ = together(summary_weight.T, kv)
    across = lax.ppermute(weight, "xl", SWAP)
    beside = lax.ppermute(weight, "core", SWAP)
    own, q, across, beside = together(own, pack_q(mem_pos, queries), across, beside)
    weights = [weight, beside, across, lax.ppermute(across, "core", SWAP)]
    q = exchange(q, "z")
    pieces = [from_group_behind(own, PRIOR - slot) for slot in SLOTS] + [own]
    q, weights = together(q, weights)
    picked = attend_first(q, pieces, absent)

    picked = exchange(picked, "z")
    out, picked = together(attend(q, pieces, absent, 0), picked)
    def from_y_behind(a, back):
        return lax.ppermute(a, "y", [(i, (i + back) % N_Y) for i in range(N_Y)])

    low = picked[: N_Z // 2]
    next_to = [from_y_behind(picked, 1), from_y_behind(picked, 3), from_y_behind(low, 2)]
    sent = [exchange(out, "z")]
    for part in range(1, CALLS):
        out, sent = together(attend(q, pieces, absent, part), sent)
        if part == CALLS - 1:
            out, next_to, picked = together(out, next_to, picked)
        sent = sent + [exchange(out, "z")]
    high = picked[N_Z // 2 :]
    rows = [picked, next_to[0], next_to[2], from_y_behind(high, 2), next_to[1]]
    summary = summarize(jnp.stack((y, xl, core)), rows, norm_gain, weights)
    sent, summary = together(sent, summary)
    return unpack(sent), summary.T


def solution(mesh):
    split = Mesh(mesh.devices.reshape(-1, N_Y, N_Z, 2, 2), ("file", "y", "z", "xl", "core"))
    tokens = ("file", "xl", "core", "y", "z")
    return jax.shard_map(
        on_device,
        mesh=split,
        in_specs=(
            P(tokens, None),
            P(tokens, None),
            P(tokens, None),
            P(tokens),
            P(),
            P(("xl", "core"), ("y", "z")),
        ),
        out_specs=(P(tokens, None), P(("file", "xl", "core"), ("y", "z"))),
        check_vma=False,
    )
```
